32 devices in a mesh: section: 4 (over z), seq: 8 (over y, x, core).
Axes of the slice: x: 2, y: 2, z: 4, core: 2. Of those that a mesh axis runs over, the one named last changes fastest.
Arguments:
- queries: bfloat16 [4, 1024, 8192], P('section', 'seq'), may hold values from -24 to 24
- keys: bfloat16 [4, 1024, 1024], P('section', 'seq'), may hold values from -24 to 24
- values: bfloat16 [4, 1024, 1024], P('section', 'seq'), may hold values from -6 to 6
- block_mask: int32 [4, 8, 8], P('section'), may hold values from 0 to 1, as said below
- block_live: int32 [4, 8], P('section'), may hold values from 1 to 128, as said below
Outputs:
- passed_context: bfloat16 [4, 1024, 8192], P('section', 'seq')
The draws below stay inside these ranges and needn't reach their ends.
Inputs may be any that keep to these rules, and one draw needn't show every extreme that they name: block_mask[m, i, j] is 1 exactly when block j is block i or one of its ancestors in micro-batch m's tree: the first 4 blocks form a chain, each later block hangs below the chain's last block or a later block of lower index. `block_live`: the first 4 blocks of every micro-batch are full, its last block holds one live token.
All inputs are finite; a program needn't handle non-finite values.
Results may differ from the reference program's by a relative error of at most 0.0049.
Values may be sent and summed in bfloat16 or wider, within the bound.
No kernel may reach another device: no remote copies, remote signals or barrier semaphores. Data moves between devices by JAX's collectives and lax.ppermute only.
A program may use at most 128 MiB of HBM per device.

```python
import jax
import jax.numpy as jnp
from jax import lax

QUERY_HEADS = 64
KEY_VALUE_HEADS = 8
HEAD_SIZE = 128
BLK = 128
MICRO_BATCHES = 4
MICRO_SLOTS = 1024
NB = 8


def draw_queries(key, part):
    array_shape = (MICRO_BATCHES, MICRO_SLOTS, QUERY_HEADS * HEAD_SIZE)
    base = jnp.clip(jax.random.normal(jax.random.fold_in(key, 1), array_shape, jnp.float32), -6.0, 6.0)
    return base.astype(jnp.bfloat16)


def draw_keys(key, part):
    array_shape = (MICRO_BATCHES, MICRO_SLOTS, KEY_VALUE_HEADS * HEAD_SIZE)
    base = jnp.clip(jax.random.normal(jax.random.fold_in(key, 2), array_shape, jnp.float32), -6.0, 6.0)
    return base.astype(jnp.bfloat16)


def draw_block_mask(key, part):
    half = NB // 2
    index = jnp.arange(NB, dtype=jnp.int32)
    raw = jax.random.randint(jax.random.fold_in(key, 21), (MICRO_BATCHES, NB), 0, 1 << 20)
    spread = jnp.maximum(index - half + 1, 1)
    parent = jnp.where(index < half, index - 1, half - 1 + raw % spread[None, :])

    def step(block, ancestry):
        parent_now = parent[:, block]
        inherited = jnp.take_along_axis(ancestry, jnp.maximum(parent_now, 0)[:, None, None], axis=1)[:, 0, :]
        inherited = jnp.where((parent_now >= 0)[:, None], inherited, 0)
        own = (index == block).astype(jnp.int32)[None, :]
        return ancestry.at[:, block, :].set(jnp.maximum(inherited, own))
    return lax.fori_loop(0, NB, step, jnp.zeros((MICRO_BATCHES, NB, NB), jnp.int32))


def draw_block_live(key, part):
    index = jnp.arange(NB, dtype=jnp.int32)
    counts = jax.random.randint(jax.random.fold_in(key, 31), (MICRO_BATCHES, NB), 1, BLK + 1)
    counts = jnp.where(index[None, :] < NB // 2, BLK, counts)
    counts = jnp.where(index[None, :] == NB - 1, 1, counts)
    return counts.astype(jnp.int32)


def block_levels(rng, shape, cuts, low, high):
    def one(dim, blocks):
        steps = jax.random.uniform(jax.random.fold_in(jax.random.fold_in(rng, 6), dim), (blocks,), jnp.float32, low / len(cuts), high / len(cuts))
        return jnp.repeat(jnp.exp(steps), shape[dim] // blocks).reshape((-1,) + (1,) * (len(shape) - dim - 1))

    factor_of = one(*cuts[0])
    for cut in cuts[1:]:
        factor_of = factor_of * one(*cut)
    return factor_of


def normal_values(own_key, shape, scale, limit, split=(), held_as=jnp.bfloat16):
    entries = scale * jax.random.normal(own_key, shape, jnp.float32)
    if split:
        entries = entries * block_levels(own_key, shape, split, -0.22, 0.18)
    return jnp.clip(entries, -limit, limit).astype(held_as)


def setup_inputs(seed: int = 0) -> dict:
    streams_of = jax.random.split(jax.random.key(seed), 6)
    queries = draw_queries(jax.random.fold_in(streams_of[5], 71), 0)
    keys = draw_keys(jax.random.fold_in(streams_of[5], 71), 0)
    values = normal_values(streams_of[2], (MICRO_BATCHES, MICRO_SLOTS, KEY_VALUE_HEADS * HEAD_SIZE), 1.0, 6.0, ((0, 4), (1, 8)))
    block_mask = draw_block_mask(jax.random.fold_in(streams_of[5], 71), 0)
    block_live = draw_block_live(jax.random.fold_in(streams_of[5], 71), 0)
    return dict(queries=queries, keys=keys, values=values, block_mask=block_mask, block_live=block_live)


def attend(qrows, qpos, keys_h, values_h, block_mask, block_live):
    total = keys_h.shape[0]
    nblk = block_mask.shape[0]
    width = total // nblk
    kpos = jnp.arange(total, dtype=jnp.int32)
    kblock = kpos // width
    key_live = (kpos % width) < jnp.repeat(block_live, width)
    qblock = qpos // width
    pick = (qblock[:, None] == jnp.arange(nblk, dtype=jnp.int32)[None, :]).astype(jnp.float32)
    allowed = jnp.repeat(jnp.dot(pick, block_mask.astype(jnp.float32)) > 0.5, width, axis=1)
    allowed = allowed & key_live[None, :] & ((kblock[None, :] != qblock[:, None]) | (kpos[None, :] <= qpos[:, None]))
    q_live = (qpos % width).astype(jnp.float32) < jnp.dot(pick, block_live.astype(jnp.float32))
    scale = qrows.shape[-1] ** -0.5
    scores = jnp.einsum("rgd,kd->grk", qrows.astype(jnp.float32), keys_h.astype(jnp.float32)) * scale
    scores = jnp.where(allowed[None], scores, -1e30)
    top = jnp.max(scores, axis=-1, keepdims=True)
    expo = jnp.where(allowed[None], jnp.exp(scores - top), 0.0)
    weights = (expo / jnp.sum(expo, axis=-1, keepdims=True)).astype(jnp.bfloat16)
    context = jnp.einsum("grk,kd->rgd", weights.astype(jnp.float32), values_h.astype(jnp.float32))
    return jnp.where(q_live[:, None, None], context, 0.0).astype(jnp.bfloat16)


def reference(queries, keys, values, block_mask, block_live):
    query_group_size = QUERY_HEADS // KEY_VALUE_HEADS

    def micro(items):
        single_query, single_key, single_value, mask_one, live_one = items
        query_head_rows = single_query.reshape(MICRO_SLOTS, KEY_VALUE_HEADS, query_group_size, HEAD_SIZE).transpose(1, 0, 2, 3)
        key_head_rows = single_key.reshape(MICRO_SLOTS, KEY_VALUE_HEADS, HEAD_SIZE).transpose(1, 0, 2)
        value_head_rows = single_value.reshape(MICRO_SLOTS, KEY_VALUE_HEADS, HEAD_SIZE).transpose(1, 0, 2)

        def head(hitems):
            q_group, k_head, v_head = hitems
            q_blocks = q_group.reshape(NB, BLK, query_group_size, HEAD_SIZE)
            starts = jnp.arange(NB, dtype=jnp.int32) * BLK

            def block_fn(bitems):
                return attend(bitems[0], bitems[1] + jnp.arange(BLK, dtype=jnp.int32), k_head, v_head, mask_one, live_one)

            return lax.map(block_fn, (q_blocks, starts)).reshape(MICRO_SLOTS, query_group_size, HEAD_SIZE)

        out = lax.map(head, (query_head_rows, key_head_rows, value_head_rows))
        return out.transpose(1, 0, 2, 3).reshape(MICRO_SLOTS, QUERY_HEADS * HEAD_SIZE)

    results = lax.map(micro, (queries, keys, values, block_mask, block_live))
    return jnp.roll(results, 1, axis=0)
```

```python
import functools

import jax
import jax.numpy as jnp
from jax import lax
from jax.experimental import pallas as pl
from jax.experimental.pallas import tpu as pltpu
from jax.sharding import PartitionSpec as P

HEAD_SIZE = 128
NEG = -1e30
COST = pl.CostEstimate(flops=1, bytes_accessed=1, transcendentals=0)


def attend_kernel(scale, mask, live, q_ref, kv_ref, o_ref, bias, scores, peak, total):
    rows = q_ref.shape[0]
    group = q_ref.shape[1] // HEAD_SIZE
    blocks = [kv_ref.at[j] for j in range(kv_ref.shape[0])]
    width = blocks[0].shape[0]
    span = 2 * width
    me = lax.axis_index("seq")
    allowed = [mask[me, b] for b in range(len(blocks))]
    pairs = range(len(blocks) // 2)
    needed = [allowed[2 * t] + allowed[2 * t + 1] > 0 for t in pairs]

    @pl.when(pl.program_id(0) == 0)
    def _():
        row = lax.broadcasted_iota(jnp.int32, (rows, width), 0)
        col = lax.broadcasted_iota(jnp.int32, (rows, width), 1)
        for p in range(len(blocks)):
            limit = jnp.where(allowed[p] == 1, live[p], 0)
            reach = jnp.where(p == me, row, rows)
            bias[:, p * width : (p + 1) * width] = jnp.where(
                (col < limit) & (col <= reach), 0.0, NEG
            )

    peak[...] = jnp.full_like(peak, NEG)
    total[...] = jnp.zeros_like(total)
    for t in pairs:

        @pl.when(needed[t])
        def _():
            q = jnp.concatenate(
                [q_ref[:, g * HEAD_SIZE : (g + 1) * HEAD_SIZE] for g in range(group)], axis=0
            )
            keys = jnp.concatenate(
                [blocks[2 * t][:, :HEAD_SIZE], blocks[2 * t + 1][:, :HEAD_SIZE]], axis=0
            )
            part = lax.dot_general(
                q, keys, (((1,), (1,)), ((), ())), preferred_element_type=jnp.float32
            )
            part = part.reshape(group, rows, span) + bias[:, t * span : (t + 1) * span][None]
            part = part.reshape(group * rows, span)
            scores[:, t * span : (t + 1) * span] = part
            here = jnp.maximum(part[:, :width], part[:, width:])
            peak[...] = jnp.maximum(peak[...], here)

    top = jnp.max(peak[...], axis=1, keepdims=True)
    peak[...] = jnp.broadcast_to(top, peak.shape)
    for t in pairs:

        @pl.when(needed[t])
        def _():
            highest = jnp.concatenate([peak[...], peak[...]], axis=1)
            expo = jnp.exp2((scores[:, t * span : (t + 1) * span] - highest) * scale)
            vals = jnp.concatenate(
                [blocks[2 * t][:, HEAD_SIZE:], blocks[2 * t + 1][:, HEAD_SIZE:]], axis=0
            )
            both = jnp.concatenate([vals, jnp.ones((span, HEAD_SIZE), jnp.bfloat16)], axis=1)
            total[...] += jnp.dot(
                expo.astype(jnp.bfloat16), both, preferred_element_type=jnp.float32
            )

    alive = lax.broadcasted_iota(jnp.int32, (rows, HEAD_SIZE), 0) < live[me]
    for g in range(group):
        one = total[g * rows : (g + 1) * rows]
        out = jnp.where(alive, one[:, :HEAD_SIZE] / one[:, HEAD_SIZE:], 0.0)
        o_ref[:, g * HEAD_SIZE : (g + 1) * HEAD_SIZE] = out.astype(jnp.bfloat16)


def attend(mask, live, queries, first, heads, group, kv):
    rows = queries.shape[0]
    count, width = kv.shape[:2]
    step = group * HEAD_SIZE
    scale = HEAD_SIZE**-0.5 * 1.4426950408889634
    smem = pl.BlockSpec(memory_space=pltpu.SMEM)
    return pl.pallas_call(
        functools.partial(attend_kernel, scale),
        grid=(heads,),
        out_shape=jax.ShapeDtypeStruct((rows, heads * step), jnp.bfloat16),
        in_specs=[
            smem,
            smem,
            pl.BlockSpec((rows, step), lambda h: (0, first + h)),
            pl.BlockSpec((count, width, 2 * HEAD_SIZE), lambda h: (0, 0, h)),
        ],
        out_specs=pl.BlockSpec((rows, step), lambda h: (0, h)),
        scratch_shapes=[
            pltpu.VMEM((rows, count * width), jnp.float32),
            pltpu.VMEM((group * rows, count * width), jnp.float32),
            pltpu.VMEM((group * rows, width), jnp.float32),
            pltpu.VMEM((group * rows, 2 * HEAD_SIZE), jnp.float32),
        ],
        compiler_params=pltpu.CompilerParams(vmem_limit_bytes=40 * 2**20),
        cost_estimate=COST,
    )(mask, live, queries, kv)


def planar_kernel(scale, mask, live, q_ref, mine, theirs, o_ref):
    rows = q_ref.shape[0]
    group = q_ref.shape[1] // HEAD_SIZE
    chips, width = mine.shape[:2]
    me = lax.axis_index("seq")
    chip, core = me // 2, me % 2

    def body(n):
        slot = lax.broadcasted_iota(jnp.int32, (width, HEAD_SIZE), 0)
        zeroth = jnp.where(
            core == 0,
            mine[n - 1, :1, :HEAD_SIZE].astype(jnp.float32),
            theirs[n - 1, :1, :HEAD_SIZE].astype(jnp.float32),
        )
        zeroth = jnp.broadcast_to(zeroth, (width, HEAD_SIZE)).astype(jnp.bfloat16)
        keys, vals = [], []
        for j in range(n):
            r = (n - 1) ^ j
            for ref, block in ((mine, 2 * j + core), (theirs, 2 * j + 1 - core)):
                there = slot < jnp.where(mask[me, block] == 1, live[block], 0)
                if r == 0 and ref is mine:
                    keys.append(ref[r, :, :HEAD_SIZE])
                else:
                    keys.append(jnp.where(there, ref[r, :, :HEAD_SIZE], zeroth))
                vals.append(
                    jnp.concatenate(
                        [
                            jnp.where(there, ref[r, :, HEAD_SIZE:], jnp.bfloat16(0)),
                            jnp.where(there, jnp.bfloat16(1), jnp.bfloat16(0)),
                        ],
                        axis=1,
                    )
                )
        pairs = [jnp.concatenate(keys[2 * j : 2 * j + 2], axis=0) for j in range(n)]
        vals = jnp.concatenate(vals, axis=0)
        row = lax.broadcasted_iota(jnp.int32, (rows, width), 0)
        col = lax.broadcasted_iota(jnp.int32, (rows, width), 1)
        bias = jnp.where((col < live[me]) & (col <= row), 0.0, NEG)
        alive = lax.broadcasted_iota(jnp.int32, (rows, HEAD_SIZE), 0) < live[me]
        for g in range(group):
            cols = slice(g * HEAD_SIZE, (g + 1) * HEAD_SIZE)
            q = q_ref[:, cols]
            scores = []
            for j in range(n):
                part = lax.dot_general(
                    q, pairs[j], (((1,), (1,)), ((), ())), preferred_element_type=jnp.float32
                )
                own, other = part[:, :width], part[:, width:]
                scores += [own + bias if j == n - 1 else own, other]
            top = functools.reduce(jnp.maximum, scores)
            top = jnp.max(top, axis=1, keepdims=True)
            expo = [jnp.exp2((one - top) * scale).astype(jnp.bfloat16) for one in scores]
            out = jnp.dot(jnp.concatenate(expo, axis=1), vals, preferred_element_type=jnp.float32)
            out = jnp.where(alive, out[:, :HEAD_SIZE] / out[:, HEAD_SIZE:], 0.0)
            o_ref[:, cols] = out.astype(jnp.bfloat16)

    for n in range(1, chips + 1):
        pl.when(chip == n - 1)(functools.partial(body, n))


def attend_planar(mask, live, queries, first, heads, group, mine, theirs):
    rows = queries.shape[0]
    step = group * HEAD_SIZE
    smem = pl.BlockSpec(memory_space=pltpu.SMEM)
    kv = pl.BlockSpec(mine.shape[:2] + (2 * HEAD_SIZE,), lambda h: (0, 0, h))
    return pl.pallas_call(
        functools.partial(planar_kernel, HEAD_SIZE**-0.5 * 1.4426950408889634),
        grid=(heads,),
        out_shape=jax.ShapeDtypeStruct((rows, heads * step), jnp.bfloat16),
        in_specs=[smem, smem, pl.BlockSpec((rows, step), lambda h: (0, first + h)), kv, kv],
        out_specs=pl.BlockSpec((rows, step), lambda h: (0, h)),
        compiler_params=pltpu.CompilerParams(vmem_limit_bytes=40 * 2**20),
        cost_estimate=COST,
    )(mask, live, queries, mine, theirs)


def pack_kernel(mask, live, q_ref, k_ref, v_ref, sent, *o_refs):
    sent[:, : q_ref.shape[1]] = q_ref[...]
    sent[:, sent.shape[1] - HEAD_SIZE :] = jnp.zeros_like(sent[:, :HEAD_SIZE])
    blocks = live.shape[0]
    deep = 16
    row = lax.broadcasted_iota(jnp.int32, (deep, HEAD_SIZE), 0)
    col = lax.broadcasted_iota(jnp.int32, (deep, HEAD_SIZE), 1)
    tile = jnp.zeros((deep, HEAD_SIZE), jnp.int32)
    for j in range(blocks):
        tile = jnp.where((row == blocks) & (col == j), live[j], tile)
        for i in range(blocks):
            tile = jnp.where((row == i) & (col == j), mask[i, j], tile)
    sent[:deep, sent.shape[1] - HEAD_SIZE :] = tile.astype(jnp.float32).astype(sent.dtype)
    head = 0
    for n, ref in enumerate((sent,) + o_refs):
        begin = 0 if n else q_ref.shape[1]
        end = ref.shape[1] if n else ref.shape[1] - HEAD_SIZE
        for at in range(begin, end, 2 * HEAD_SIZE):
            cols = slice(head * HEAD_SIZE, (head + 1) * HEAD_SIZE)
            ref[:, at : at + HEAD_SIZE] = k_ref[:, cols]
            ref[:, at + HEAD_SIZE : at + 2 * HEAD_SIZE] = v_ref[:, cols]
            head += 1


def pack(mask, live, queries, keys, values, heads):
    rows, cols = keys.shape
    width = heads * 2 * HEAD_SIZE
    count = cols // (heads * HEAD_SIZE) - 1
    q_cols = heads * HEAD_SIZE * queries.shape[1] // cols
    smem = pl.BlockSpec(memory_space=pltpu.SMEM)

    def whole(shape):
        return pl.BlockSpec(shape, lambda i: (0, 0))

    shapes = [(rows, q_cols + width + HEAD_SIZE)] + [(rows, width)] * count
    return pl.pallas_call(
        pack_kernel,
        grid=(1,),
        out_shape=[jax.ShapeDtypeStruct(shape, keys.dtype) for shape in shapes],
        in_specs=[smem, smem, whole((rows, q_cols)), whole(keys.shape), whole(values.shape)],
        out_specs=[whole(shape) for shape in shapes],
        cost_estimate=COST,
    )(mask, live, queries, keys, values)


def pack_pairs(keys, values, heads):
    parts = []
    for h in heads:
        cols = slice(h * HEAD_SIZE, (h + 1) * HEAD_SIZE)
        parts += [keys[:, cols], values[:, cols]]
    return jnp.concatenate(parts, axis=1)


def after(value, *others):
    return lax.optimization_barrier((value,) + others)[0]


def on_plane(nsec, to):
    return [(s * 8 + i, s * 8 + to(i)) for s in range(nsec) for i in range(8)]


def exchange(part, nsec, by):
    return lax.ppermute(part, ("section", "seq"), on_plane(nsec, lambda i: i ^ by))


def per_device_8(queries, keys, values, block_mask, block_live):
    nsec = lax.axis_size("section")
    group = queries.shape[2] // keys.shape[2]
    step = group * HEAD_SIZE
    q, k, v = queries[0], keys[0], values[0]
    mask, live = block_mask[0], block_live[0]
    onward = [(i, (i + 1) % nsec) for i in range(nsec)]

    def on(value):
        return lax.ppermute(value, "section", onward)

    sent, *parts = pack(mask, live, q, k, v, 2)
    got = on(sent)

    def gather(part):
        return jnp.stack([part] + [exchange(part, nsec, by) for by in (2, 4, 6)])

    def both_cores(mine):
        return mine, exchange(mine, nsec, 1)

    def run(mask, live, q, first, kvs):
        return attend_planar(mask, live, q, first, 2, group, *kvs)

    mine1 = gather(parts[0])
    part2 = after(parts[1], mine1)
    ctx1 = run(mask, live, q, 2, both_cores(mine1))
    out1 = on(ctx1)
    mine2 = after(gather(part2), ctx1, got)
    part3 = after(parts[2], mine2)
    ctx2 = run(mask, live, q, 4, both_cores(mine2))
    out2 = on(ctx2)
    mine3 = after(gather(part3), ctx2, out1)
    part0 = after(got[:, 2 * step : -HEAD_SIZE], mine3)
    ctx3 = run(mask, live, q, 6, both_cores(mine3))
    out3 = on(ctx3)
    kvs0 = both_cores(after(gather(part0), ctx3, out2))
    blocks = live.shape[0]
    tab = got[: blocks + 1, -HEAD_SIZE:][:, :blocks].astype(jnp.int32)
    first = run(tab[:-1], tab[-1], got, 0, kvs0)
    return jnp.concatenate([first, out1, out2, out3], axis=1)[None]


def per_device(queries, keys, values, block_mask, block_live):
    nsec = lax.axis_size("section")
    group = queries.shape[2] // keys.shape[2]
    onward = [(i, (i + 1) % nsec) for i in range(nsec)]
    outs = []
    for h in range(0, keys.shape[2] // HEAD_SIZE, 2):
        kv = lax.all_gather(pack_pairs(keys[0], values[0], [h, h + 1]), "seq", axis=0)
        out = attend(block_mask[0], block_live[0], queries[0], h, 2, group, kv)
        outs.append(lax.ppermute(out, "section", onward))
    return jnp.concatenate(outs, axis=1)[None]


def solution(mesh):
    placed = (
        P("section", "seq", None),
        P("section", "seq", None),
        P("section", "seq", None),
        P("section", None, None),
        P("section", None),
    )
    body = per_device_8 if mesh.shape["seq"] == 8 else per_device
    return jax.shard_map(
        body, mesh=mesh, in_specs=placed, out_specs=P("section", "seq", None), check_vma=False
    )
```

```python
import functools

import jax
import jax.numpy as jnp
from jax import lax
from jax.experimental import pallas as pl
from jax.experimental.pallas import tpu as pltpu
from jax.sharding import PartitionSpec as P

HEAD_SIZE = 128
NEG = -1e30
COST = pl.CostEstimate(flops=1, bytes_accessed=1, transcendentals=0)


def attend_kernel(scale, mask, live, q_ref, kv_ref, o_ref, bias, scores, peak, total):
    rows = q_ref.shape[0]
    group = q_ref.shape[1] // HEAD_SIZE
    blocks = [kv_ref.at[j] for j in range(kv_ref.shape[0])]
    width = blocks[0].shape[0]
    span = 2 * width
    me = lax.axis_index("seq")
    allowed = [mask[me, b] for b in range(len(blocks))]
    pairs = range(len(blocks) // 2)
    needed = [allowed[2 * t] + allowed[2 * t + 1] > 0 for t in pairs]

    @pl.when(pl.program_id(0) == 0)
    def _():
        row = lax.broadcasted_iota(jnp.int32, (rows, width), 0)
        col = lax.broadcasted_iota(jnp.int32, (rows, width), 1)
        for p in range(len(blocks)):
            limit = jnp.where(allowed[p] == 1, live[p], 0)
            reach = jnp.where(p == me, row, rows)
            bias[:, p * width : (p + 1) * width] = jnp.where(
                (col < limit) & (col <= reach), 0.0, NEG
            )

    peak[...] = jnp.full_like(peak, NEG)
    total[...] = jnp.zeros_like(total)
    for t in pairs:

        @pl.when(needed[t])
        def _():
            q = jnp.concatenate(
                [q_ref[:, g * HEAD_SIZE : (g + 1) * HEAD_SIZE] for g in range(group)], axis=0
            )
            keys = jnp.concatenate(
                [blocks[2 * t][:, :HEAD_SIZE], blocks[2 * t + 1][:, :HEAD_SIZE]], axis=0
            )
            part = lax.dot_general(
                q, keys, (((1,), (1,)), ((), ())), preferred_element_type=jnp.float32
            )
            part = part.reshape(group, rows, span) + bias[:, t * span : (t + 1) * span][None]
            part = part.reshape(group * rows, span)
            scores[:, t * span : (t + 1) * span] = part
            here = jnp.maximum(part[:, :width], part[:, width:])
            peak[...] = jnp.maximum(peak[...], here)

    top = jnp.max(peak[...], axis=1, keepdims=True)
    peak[...] = jnp.broadcast_to(top, peak.shape)
    for t in pairs:

        @pl.when(needed[t])
        def _():
            highest = jnp.concatenate([peak[...], peak[...]], axis=1)
            expo = jnp.exp2((scores[:, t * span : (t + 1) * span] - highest) * scale)
            vals = jnp.concatenate(
                [blocks[2 * t][:, HEAD_SIZE:], blocks[2 * t + 1][:, HEAD_SIZE:]], axis=0
            )
            both = jnp.concatenate([vals, jnp.ones((span, HEAD_SIZE), jnp.bfloat16)], axis=1)
            total[...] += jnp.dot(
                expo.astype(jnp.bfloat16), both, preferred_element_type=jnp.float32
            )

    alive = lax.broadcasted_iota(jnp.int32, (rows, HEAD_SIZE), 0) < live[me]
    for g in range(group):
        one = total[g * rows : (g + 1) * rows]
        out = jnp.where(alive, one[:, :HEAD_SIZE] / one[:, HEAD_SIZE:], 0.0)
        o_ref[:, g * HEAD_SIZE : (g + 1) * HEAD_SIZE] = out.astype(jnp.bfloat16)


def attend(mask, live, queries, first, heads, group, kv):
    rows = queries.shape[0]
    count, width = kv.shape[:2]
    step = group * HEAD_SIZE
    scale = HEAD_SIZE**-0.5 * 1.4426950408889634
    smem = pl.BlockSpec(memory_space=pltpu.SMEM)
    return pl.pallas_call(
        functools.partial(attend_kernel, scale),
        grid=(heads,),
        out_shape=jax.ShapeDtypeStruct((rows, heads * step), jnp.bfloat16),
        in_specs=[
            smem,
            smem,
            pl.BlockSpec((rows, step), lambda h: (0, first + h)),
            pl.BlockSpec((count, width, 2 * HEAD_SIZE), lambda h: (0, 0, h)),
        ],
        out_specs=pl.BlockSpec((rows, step), lambda h: (0, h)),
        scratch_shapes=[
            pltpu.VMEM((rows, count * width), jnp.float32),
            pltpu.VMEM((group * rows, count * width), jnp.float32),
            pltpu.VMEM((group * rows, width), jnp.float32),
            pltpu.VMEM((group * rows, 2 * HEAD_SIZE), jnp.float32),
        ],
        compiler_params=pltpu.CompilerParams(vmem_limit_bytes=40 * 2**20),
        cost_estimate=COST,
    )(mask, live, queries, kv)


def planar_kernel(scale, mask, live, q_ref, mine, theirs, o_ref):
    rows = q_ref.shape[0]
    group = q_ref.shape[1] // HEAD_SIZE
    chips, width = mine.shape[:2]
    me = lax.axis_index("seq")
    chip, core = me // 2, me % 2

    def body(n):
        slot = lax.broadcasted_iota(jnp.int32, (width, HEAD_SIZE), 0)
        zeroth = jnp.where(
            core == 0,
            mine[n - 1, :1, :HEAD_SIZE].astype(jnp.float32),
            theirs[n - 1, :1, :HEAD_SIZE].astype(jnp.float32),
        )
        zeroth = jnp.broadcast_to(zeroth, (width, HEAD_SIZE)).astype(jnp.bfloat16)
        keys, vals = [], []
        for j in range(n):
            r = (n - 1) ^ j
            for ref, block in ((mine, 2 * j + core), (theirs, 2 * j + 1 - core)):
                there = slot < jnp.where(mask[me, block] == 1, live[block], 0)
                if r == 0 and ref is mine:
                    keys.append(ref[r, :, :HEAD_SIZE])
                else:
                    keys.append(jnp.where(there, ref[r, :, :HEAD_SIZE], zeroth))
                vals.append(
                    jnp.concatenate(
                        [
                            jnp.where(there, ref[r, :, HEAD_SIZE:], jnp.bfloat16(0)),
                            jnp.where(there, jnp.bfloat16(1), jnp.bfloat16(0)),
                        ],
                        axis=1,
                    )
                )
        pairs = [jnp.concatenate(keys[2 * j : 2 * j + 2], axis=0) for j in range(n)]
        vals = jnp.concatenate(vals, axis=0)
        row = lax.broadcasted_iota(jnp.int32, (rows, width), 0)
        col = lax.broadcasted_iota(jnp.int32, (rows, width), 1)
        bias = jnp.where((col < live[me]) & (col <= row), 0.0, NEG)
        alive = lax.broadcasted_iota(jnp.int32, (rows, HEAD_SIZE), 0) < live[me]
        for g in range(group):
            cols = slice(g * HEAD_SIZE, (g + 1) * HEAD_SIZE)
            q = q_ref[:, cols]
            scores = []
            for j in range(n):
                part = lax.dot_general(
                    q, pairs[j], (((1,), (1,)), ((), ())), preferred_element_type=jnp.float32
                )
                own, other = part[:, :width], part[:, width:]
                scores += [own + bias if j == n - 1 else own, other]
            top = functools.reduce(jnp.maximum, scores)
            top = jnp.max(top, axis=1, keepdims=True)
            expo = [jnp.exp2((one - top) * scale).astype(jnp.bfloat16) for one in scores]
            out = jnp.dot(jnp.concatenate(expo, axis=1), vals, preferred_element_type=jnp.float32)
            out = jnp.where(alive, out[:, :HEAD_SIZE] / out[:, HEAD_SIZE:], 0.0)
            o_ref[:, cols] = out.astype(jnp.bfloat16)

    for n in range(1, chips + 1):
        pl.when(chip == n - 1)(functools.partial(body, n))


def attend_planar(mask, live, queries, q_first, group, kvs, kv_first, heads):
    rows = queries.shape[0]
    step = group * HEAD_SIZE
    smem = pl.BlockSpec(memory_space=pltpu.SMEM)
    mine, theirs = kvs
    kv = pl.BlockSpec(mine.shape[:2] + (2 * HEAD_SIZE,), lambda i: (0, 0, kv_first + i))
    return pl.pallas_call(
        functools.partial(planar_kernel, HEAD_SIZE**-0.5 * 1.4426950408889634),
        grid=(heads,),
        out_shape=jax.ShapeDtypeStruct((rows, heads * step), jnp.bfloat16),
        in_specs=[smem, smem, pl.BlockSpec((rows, step), lambda i: (0, q_first + i)), kv, kv],
        out_specs=pl.BlockSpec((rows, step), lambda i: (0, i)),
        compiler_params=pltpu.CompilerParams(vmem_limit_bytes=40 * 2**20),
        cost_estimate=COST,
    )(mask, live, queries, mine, theirs)


def pack_heads(k_ref, v_ref, first, ref, count):
    for i in range(count):
        cols = slice((first + i) * HEAD_SIZE, (first + i + 1) * HEAD_SIZE)
        ref[:, 2 * i * HEAD_SIZE : (2 * i + 1) * HEAD_SIZE] = k_ref[:, cols]
        ref[:, (2 * i + 1) * HEAD_SIZE : (2 * i + 2) * HEAD_SIZE] = v_ref[:, cols]


def ahead_kernel(heads, mask, live, k_ref, v_ref, sent):
    pack_heads(k_ref, v_ref, 0, sent, heads)
    last = sent.shape[1] - HEAD_SIZE
    sent[:, last:] = jnp.zeros_like(sent[:, last:])
    blocks = live.shape[0]
    deep = 16
    row = lax.broadcasted_iota(jnp.int32, (deep, HEAD_SIZE), 0)
    col = lax.broadcasted_iota(jnp.int32, (deep, HEAD_SIZE), 1)
    tile = jnp.zeros((deep, HEAD_SIZE), jnp.int32)
    for j in range(blocks):
        tile = jnp.where((row == blocks) & (col == j), live[j], tile)
        for i in range(blocks):
            tile = jnp.where((row == i) & (col == j), mask[i, j], tile)
    sent[:deep, last:] = tile.astype(jnp.float32).astype(sent.dtype)


def whole(shape):
    return pl.BlockSpec(shape, lambda i: (0, 0))


def pack_ahead(mask, live, keys, values, heads):
    rows = keys.shape[0]
    smem = pl.BlockSpec(memory_space=pltpu.SMEM)
    shape = (rows, heads * 2 * HEAD_SIZE + HEAD_SIZE)
    kv = whole((rows, heads * HEAD_SIZE))
    return pl.pallas_call(
        functools.partial(ahead_kernel, heads),
        grid=(1,),
        out_shape=jax.ShapeDtypeStruct(shape, keys.dtype),
        in_specs=[smem, smem, kv, kv],
        out_specs=whole(shape),
        cost_estimate=COST,
    )(mask, live, keys, values)


def rest_kernel(k_ref, v_ref, q_ref, sent, part, q_sent):
    pack_heads(k_ref, v_ref, 0, part, part.shape[1] // (2 * HEAD_SIZE))
    q_sent[...] = q_ref[...]


def pack_rest(keys, values, queries, q_cols, sent):
    rows, cols = keys.shape
    shapes = [(rows, cols), (rows, q_cols)]
    later = pl.BlockSpec((rows, cols // 2), lambda i: (0, 1))
    return pl.pallas_call(
        rest_kernel,
        grid=(1,),
        out_shape=[jax.ShapeDtypeStruct(shape, keys.dtype) for shape in shapes],
        in_specs=[later, later, whole((rows, q_cols)), pl.BlockSpec(memory_space=pl.ANY)],
        out_specs=[whole(shape) for shape in shapes],
        cost_estimate=COST,
    )(keys, values, queries, sent)


def pack_pairs(keys, values, heads):
    parts = []
    for h in heads:
        cols = slice(h * HEAD_SIZE, (h + 1) * HEAD_SIZE)
        parts += [keys[:, cols], values[:, cols]]
    return jnp.concatenate(parts, axis=1)


def after(value, *others):
    return lax.optimization_barrier((value,) + others)[0] if others else value


def on_plane(nsec, to):
    return [(s * 8 + i, s * 8 + to(i)) for s in range(nsec) for i in range(8)]


def exchange(part, nsec, by):
    return lax.ppermute(part, ("section", "seq"), on_plane(nsec, lambda i: i ^ by))


def per_device_8(queries, keys, values, block_mask, block_live):
    nsec = lax.axis_size("section")
    group = queries.shape[2] // keys.shape[2]
    step = group * HEAD_SIZE
    q, k, v = queries[0], keys[0], values[0]
    mask, live = block_mask[0], block_live[0]
    onward = [(i, (i + 1) % nsec) for i in range(nsec)]

    def on(value):
        return lax.ppermute(value, "section", onward)

    half = keys.shape[2] // HEAD_SIZE // 2
    sent = pack_ahead(mask, live, k, v, half)
    part1, q01 = pack_rest(k, v, q, 2 * step, sent)
    sent_in, q01_in = on(sent), on(q01)
    q23_in = on(q[:, 2 * step : 4 * step])

    def gather(part, *before):
        near = [exchange(part, nsec, by) for by in (2, 4)]
        return [part] + near + [exchange(after(part, *before), nsec, 6)]

    def split(pieces, count):
        width = pieces[0].shape[1] // count
        return [jnp.stack([p[:, i * width : (i + 1) * width] for p in pieces]) for i in range(count)]

    def swapped(mines):
        if len(mines) == 1:
            return mines[0], exchange(mines[0], nsec, 1)
        return jnp.concatenate(mines, axis=2), jnp.concatenate([exchange(m, nsec, 1) for m in mines], axis=2)

    mines1 = split(gather(part1, sent_in), 4)
    mines1 = lax.optimization_barrier((*mines1, q01_in))[:4]
    kvs1 = swapped(mines1)
    ctx = attend_planar(mask, live, q, half, group, kvs1, 0, half)
    out = on(ctx)
    part0 = after(sent_in[:, :-HEAD_SIZE], mines1[0])
    pieces0 = gather(part0, ctx)
    blocks = live.shape[0]
    tab = sent_in[: blocks + 1, -HEAD_SIZE:][:, :blocks].astype(jnp.int32)
    mask_in, live_in = tab[:-1], tab[-1]
    mines0 = split(pieces0, 4)
    mines0 = lax.optimization_barrier((*mines0, q23_in, ctx))[:4]
    theirs0 = [exchange(m, nsec, 1) for m in mines0]
    heads = half // 4
    ins = []
    for i, kvs in enumerate(zip(mines0, theirs0)):
        at = i * heads
        q_in = q01_in if at < 2 else q23_in
        ins.append(attend_planar(mask_in, live_in, q_in, at % 2, group, kvs, 0, heads))
    return jnp.concatenate(ins + [out], axis=1)[None]


def per_device(queries, keys, values, block_mask, block_live):
    nsec = lax.axis_size("section")
    group = queries.shape[2] // keys.shape[2]
    onward = [(i, (i + 1) % nsec) for i in range(nsec)]
    outs = []
    for h in range(0, keys.shape[2] // HEAD_SIZE, 2):
        kv = lax.all_gather(pack_pairs(keys[0], values[0], [h, h + 1]), "seq", axis=0)
        out = attend(block_mask[0], block_live[0], queries[0], h, 2, group, kv)
        outs.append(lax.ppermute(out, "section", onward))
    return jnp.concatenate(outs, axis=1)[None]


def solution(mesh):
    placed = (
        P("section", "seq", None),
        P("section", "seq", None),
        P("section", "seq", None),
        P("section", None, None),
        P("section", None),
    )
    body = per_device_8 if mesh.shape["seq"] == 8 else per_device
    return jax.shard_map(
        body, mesh=mesh, in_specs=placed, out_specs=P("section", "seq", None), check_vma=False
    )
```

```python
import functools

import jax
import jax.numpy as jnp
from jax import lax
from jax.experimental import pallas as pl
from jax.experimental.pallas import tpu as pltpu
from jax.sharding import PartitionSpec as P

HEAD_SIZE = 128
NEG = -1e30
COST = pl.CostEstimate(flops=1, bytes_accessed=1, transcendentals=0)


def attend_kernel(scale, mask, live, q_ref, kv_ref, o_ref, bias, scores, peak, total):
    rows = q_ref.shape[0]
    group = q_ref.shape[1] // HEAD_SIZE
    blocks = [kv_ref.at[j] for j in range(kv_ref.shape[0])]
    width = blocks[0].shape[0]
    span = 2 * width
    me = lax.axis_index("seq")
    allowed = [mask[me, b] for b in range(len(blocks))]
    pairs = range(len(blocks) // 2)
    needed = [allowed[2 * t] + allowed[2 * t + 1] > 0 for t in pairs]

    @pl.when(pl.program_id(0) == 0)
    def _():
        row = lax.broadcasted_iota(jnp.int32, (rows, width), 0)
        col = lax.broadcasted_iota(jnp.int32, (rows, width), 1)
        for p in range(len(blocks)):
            limit = jnp.where(allowed[p] == 1, live[p], 0)
            reach = jnp.where(p == me, row, rows)
            bias[:, p * width : (p + 1) * width] = jnp.where(
                (col < limit) & (col <= reach), 0.0, NEG
            )

    peak[...] = jnp.full_like(peak, NEG)
    total[...] = jnp.zeros_like(total)
    for t in pairs:

        @pl.when(needed[t])
        def _():
            q = jnp.concatenate(
                [q_ref[:, g * HEAD_SIZE : (g + 1) * HEAD_SIZE] for g in range(group)], axis=0
            )
            keys = jnp.concatenate(
                [blocks[2 * t][:, :HEAD_SIZE], blocks[2 * t + 1][:, :HEAD_SIZE]], axis=0
            )
            part = lax.dot_general(
                q, keys, (((1,), (1,)), ((), ())), preferred_element_type=jnp.float32
            )
            part = part.reshape(group, rows, span) + bias[:, t * span : (t + 1) * span][None]
            part = part.reshape(group * rows, span)
            scores[:, t * span : (t + 1) * span] = part
            here = jnp.maximum(part[:, :width], part[:, width:])
            peak[...] = jnp.maximum(peak[...], here)

    top = jnp.max(peak[...], axis=1, keepdims=True)
    peak[...] = jnp.broadcast_to(top, peak.shape)
    for t in pairs:

        @pl.when(needed[t])
        def _():
            highest = jnp.concatenate([peak[...], peak[...]], axis=1)
            expo = jnp.exp2((scores[:, t * span : (t + 1) * span] - highest) * scale)
            vals = jnp.concatenate(
                [blocks[2 * t][:, HEAD_SIZE:], blocks[2 * t + 1][:, HEAD_SIZE:]], axis=0
            )
            both = jnp.concatenate([vals, jnp.ones((span, HEAD_SIZE), jnp.bfloat16)], axis=1)
            total[...] += jnp.dot(
                expo.astype(jnp.bfloat16), both, preferred_element_type=jnp.float32
            )

    alive = lax.broadcasted_iota(jnp.int32, (rows, HEAD_SIZE), 0) < live[me]
    for g in range(group):
        one = total[g * rows : (g + 1) * rows]
        out = jnp.where(alive, one[:, :HEAD_SIZE] / one[:, HEAD_SIZE:], 0.0)
        o_ref[:, g * HEAD_SIZE : (g + 1) * HEAD_SIZE] = out.astype(jnp.bfloat16)


def attend(mask, live, queries, first, heads, group, kv):
    rows = queries.shape[0]
    count, width = kv.shape[:2]
    step = group * HEAD_SIZE
    scale = HEAD_SIZE**-0.5 * 1.4426950408889634
    smem = pl.BlockSpec(memory_space=pltpu.SMEM)
    return pl.pallas_call(
        functools.partial(attend_kernel, scale),
        grid=(heads,),
        out_shape=jax.ShapeDtypeStruct((rows, heads * step), jnp.bfloat16),
        in_specs=[
            smem,
            smem,
            pl.BlockSpec((rows, step), lambda h: (0, first + h)),
            pl.BlockSpec((count, width, 2 * HEAD_SIZE), lambda h: (0, 0, h)),
        ],
        out_specs=pl.BlockSpec((rows, step), lambda h: (0, h)),
        scratch_shapes=[
            pltpu.VMEM((rows, count * width), jnp.float32),
            pltpu.VMEM((group * rows, count * width), jnp.float32),
            pltpu.VMEM((group * rows, width), jnp.float32),
            pltpu.VMEM((group * rows, 2 * HEAD_SIZE), jnp.float32),
        ],
        compiler_params=pltpu.CompilerParams(vmem_limit_bytes=40 * 2**20),
        cost_estimate=COST,
    )(mask, live, queries, kv)


def planar_kernel(scale, mask, live, q_ref, mine, theirs, o_ref):
    rows = q_ref.shape[0]
    group = q_ref.shape[1] // HEAD_SIZE
    chips, width = mine.shape[:2]
    me = lax.axis_index("seq")
    chip, core = me // 2, me % 2

    def body(n):
        slot = lax.broadcasted_iota(jnp.int32, (width, HEAD_SIZE), 0)
        zeroth = jnp.where(
            core == 0,
            mine[n - 1, :1, :HEAD_SIZE].astype(jnp.float32),
            theirs[n - 1, :1, :HEAD_SIZE].astype(jnp.float32),
        )
        zeroth = jnp.broadcast_to(zeroth, (width, HEAD_SIZE)).astype(jnp.bfloat16)
        keys, vals = [], []
        for j in range(n):
            r = (n - 1) ^ j
            for ref, block in ((mine, 2 * j + core), (theirs, 2 * j + 1 - core)):
                there = slot < jnp.where(mask[me, block] == 1, live[block], 0)
                if r == 0 and ref is mine:
                    keys.append(ref[r, :, :HEAD_SIZE])
                else:
                    keys.append(jnp.where(there, ref[r, :, :HEAD_SIZE], zeroth))
                vals.append(
                    jnp.concatenate(
                        [
                            jnp.where(there, ref[r, :, HEAD_SIZE:], jnp.bfloat16(0)),
                            jnp.where(there, jnp.bfloat16(1), jnp.bfloat16(0)),
                        ],
                        axis=1,
                    )
                )
        pairs = [jnp.concatenate(keys[2 * j : 2 * j + 2], axis=0) for j in range(n)]
        vals = jnp.concatenate(vals, axis=0)
        row = lax.broadcasted_iota(jnp.int32, (rows, width), 0)
        col = lax.broadcasted_iota(jnp.int32, (rows, width), 1)
        bias = jnp.where((col < live[me]) & (col <= row), 0.0, NEG)
        alive = lax.broadcasted_iota(jnp.int32, (rows, HEAD_SIZE), 0) < live[me]
        for g in range(group):
            cols = slice(g * HEAD_SIZE, (g + 1) * HEAD_SIZE)
            q = q_ref[:, cols]
            scores = []
            for j in range(n):
                part = lax.dot_general(
                    q, pairs[j], (((1,), (1,)), ((), ())), preferred_element_type=jnp.float32
                )
                own, other = part[:, :width], part[:, width:]
                scores += [own + bias if j == n - 1 else own, other]
            top = functools.reduce(jnp.maximum, scores)
            top = jnp.max(top, axis=1, keepdims=True)
            expo = [jnp.exp2((one - top) * scale).astype(jnp.bfloat16) for one in scores]
            out = jnp.dot(jnp.concatenate(expo, axis=1), vals, preferred_element_type=jnp.float32)
            out = jnp.where(alive, out[:, :HEAD_SIZE] / out[:, HEAD_SIZE:], 0.0)
            o_ref[:, cols] = out.astype(jnp.bfloat16)

    for n in range(1, chips + 1):
        pl.when(chip == n - 1)(functools.partial(body, n))


def attend_planar(mask, live, queries, q_first, group, kvs, kv_first, heads):
    rows = queries.shape[0]
    step = group * HEAD_SIZE
    smem = pl.BlockSpec(memory_space=pltpu.SMEM)
    mine, theirs = kvs
    kv = pl.BlockSpec(mine.shape[:2] + (2 * HEAD_SIZE,), lambda i: (0, 0, kv_first + i))
    return pl.pallas_call(
        functools.partial(planar_kernel, HEAD_SIZE**-0.5 * 1.4426950408889634),
        grid=(heads,),
        out_shape=jax.ShapeDtypeStruct((rows, heads * step), jnp.bfloat16),
        in_specs=[smem, smem, pl.BlockSpec((rows, step), lambda i: (0, q_first + i)), kv, kv],
        out_specs=pl.BlockSpec((rows, step), lambda i: (0, i)),
        compiler_params=pltpu.CompilerParams(vmem_limit_bytes=40 * 2**20),
        cost_estimate=COST,
    )(mask, live, queries, mine, theirs)


def pack_heads(k_ref, v_ref, first, ref, count):
    for i in range(count):
        cols = slice((first + i) * HEAD_SIZE, (first + i + 1) * HEAD_SIZE)
        ref[:, 2 * i * HEAD_SIZE : (2 * i + 1) * HEAD_SIZE] = k_ref[:, cols]
        ref[:, (2 * i + 1) * HEAD_SIZE : (2 * i + 2) * HEAD_SIZE] = v_ref[:, cols]


def ahead_kernel(k_ref, v_ref, sent):
    pack_heads(k_ref, v_ref, 0, sent, sent.shape[1] // (2 * HEAD_SIZE))


def pack_ahead(keys, values, heads):
    rows = keys.shape[0]
    shape = (rows, heads * 2 * HEAD_SIZE)
    kv = whole((rows, heads * HEAD_SIZE))
    return pl.pallas_call(
        ahead_kernel,
        grid=(1,),
        out_shape=jax.ShapeDtypeStruct(shape, keys.dtype),
        in_specs=[kv, kv],
        out_specs=whole(shape),
        cost_estimate=COST,
    )(keys, values)


def rest_kernel(first, mask, live, q_ref, k_ref, v_ref, sent, q_sent, part):
    pack_heads(k_ref, v_ref, first, part, part.shape[1] // (2 * HEAD_SIZE))
    last = q_ref.shape[1]
    q_sent[:, :last] = q_ref[...]
    q_sent[:, last:] = jnp.zeros_like(q_sent[:, last:])
    blocks = live.shape[0]
    deep = 16
    row = lax.broadcasted_iota(jnp.int32, (deep, HEAD_SIZE), 0)
    col = lax.broadcasted_iota(jnp.int32, (deep, HEAD_SIZE), 1)
    tile = jnp.zeros((deep, HEAD_SIZE), jnp.int32)
    for j in range(blocks):
        tile = jnp.where((row == blocks) & (col == j), live[j], tile)
        for i in range(blocks):
            tile = jnp.where((row == i) & (col == j), mask[i, j], tile)
    q_sent[:deep, last:] = tile.astype(jnp.float32).astype(q_sent.dtype)


def whole(shape):
    return pl.BlockSpec(shape, lambda i: (0, 0))


def pack_rest(mask, live, queries, keys, values, first, sent):
    rows, cols = keys.shape
    q_cols = queries.shape[1] // (cols // HEAD_SIZE) * first
    smem = pl.BlockSpec(memory_space=pltpu.SMEM)
    shapes = [(rows, q_cols + HEAD_SIZE), (rows, 2 * (cols - first * HEAD_SIZE))]
    return pl.pallas_call(
        functools.partial(rest_kernel, first),
        grid=(1,),
        out_shape=[jax.ShapeDtypeStruct(shape, keys.dtype) for shape in shapes],
        in_specs=[smem, smem, whole((rows, q_cols)), whole(keys.shape), whole(values.shape)]
        + [pl.BlockSpec(memory_space=pl.ANY)],
        out_specs=[whole(shape) for shape in shapes],
        cost_estimate=COST,
    )(mask, live, queries, keys, values, sent)


def pack_pairs(keys, values, heads):
    parts = []
    for h in heads:
        cols = slice(h * HEAD_SIZE, (h + 1) * HEAD_SIZE)
        parts += [keys[:, cols], values[:, cols]]
    return jnp.concatenate(parts, axis=1)


def after(value, *others):
    return lax.optimization_barrier((value,) + others)[0] if others else value


def on_plane(nsec, to):
    return [(s * 8 + i, s * 8 + to(i)) for s in range(nsec) for i in range(8)]


def exchange(part, nsec, by):
    return lax.ppermute(part, ("section", "seq"), on_plane(nsec, lambda i: i ^ by))


def per_device_8(queries, keys, values, block_mask, block_live):
    nsec = lax.axis_size("section")
    kv_heads = keys.shape[2] // HEAD_SIZE
    group = queries.shape[2] // keys.shape[2]
    step = group * HEAD_SIZE
    q, k, v = queries[0], keys[0], values[0]
    mask, live = block_mask[0], block_live[0]
    onward = [(i, (i + 1) % nsec) for i in range(nsec)]
    half = kv_heads // 2

    def on(value):
        return lax.ppermute(value, "section", onward)

    def gather(part, *before):
        pieces = [part] + [exchange(part, nsec, by) for by in (2, 4)]
        pieces.append(exchange(after(part, *before), nsec, 6))
        width = 2 * HEAD_SIZE
        return [jnp.stack([p[:, h * width : (h + 1) * width] for p in pieces]) for h in range(half)]

    def both_cores(mines):
        return [(mine, exchange(mine, nsec, 1)) for mine in mines]

    sent = pack_ahead(k, v, half)
    q_sent, part1 = pack_rest(mask, live, q, k, v, half, sent)
    sent_in, q_in = on(sent), on(q_sent)

    mines1 = gather(part1, sent_in)
    kvs1 = both_cores(mines1)
    ctx = [attend_planar(mask, live, q, half + h, group, kvs1[h], 0, 1) for h in range(half)]
    out = on(jnp.concatenate(ctx, axis=1))

    part0 = after(sent_in, *mines1)
    mines0 = gather(part0, ctx[0], q_in)
    mines0 = lax.optimization_barrier((*mines0, *ctx))[:half]
    kvs0 = both_cores(mines0)
    blocks = live.shape[0]
    tab = q_in[: blocks + 1, half * step :][:, :blocks].astype(jnp.int32)
    first = [attend_planar(tab[:-1], tab[-1], q_in, h, group, kvs0[h], 0, 1) for h in range(half)]
    return jnp.concatenate(first + [out], axis=1)[None]


def per_device(queries, keys, values, block_mask, block_live):
    nsec = lax.axis_size("section")
    group = queries.shape[2] // keys.shape[2]
    onward = [(i, (i + 1) % nsec) for i in range(nsec)]
    outs = []
    for h in range(0, keys.shape[2] // HEAD_SIZE, 2):
        kv = lax.all_gather(pack_pairs(keys[0], values[0], [h, h + 1]), "seq", axis=0)
        out = attend(block_mask[0], block_live[0], queries[0], h, 2, group, kv)
        outs.append(lax.ppermute(out, "section", onward))
    return jnp.concatenate(outs, axis=1)[None]


def solution(mesh):
    placed = (
        P("section", "seq", None),
        P("section", "seq", None),
        P("section", "seq", None),
        P("section", None, None),
        P("section", None),
    )
    body = per_device_8 if mesh.shape["seq"] == 8 else per_device
    return jax.shard_map(
        body, mesh=mesh, in_specs=placed, out_specs=P("section", "seq", None), check_vma=False
    )
```

```python
import functools

import jax
import jax.numpy as jnp
from jax import lax
from jax.experimental import pallas as pl
from jax.experimental.pallas import tpu as pltpu
from jax.sharding import PartitionSpec as P

HEAD_SIZE = 128
NEG = -1e30
COST = pl.CostEstimate(flops=1, bytes_accessed=1, transcendentals=0)


def attend_kernel(scale, mask, live, q_ref, kv_ref, o_ref, bias, scores, peak, total):
    rows = q_ref.shape[0]
    group = q_ref.shape[1] // HEAD_SIZE
    blocks = [kv_ref.at[j] for j in range(kv_ref.shape[0])]
    width = blocks[0].shape[0]
    span = 2 * width
    me = lax.axis_index("seq")
    allowed = [mask[me, b] for b in range(len(blocks))]
    pairs = range(len(blocks) // 2)
    needed = [allowed[2 * t] + allowed[2 * t + 1] > 0 for t in pairs]

    @pl.when(pl.program_id(0) == 0)
    def _():
        row = lax.broadcasted_iota(jnp.int32, (rows, width), 0)
        col = lax.broadcasted_iota(jnp.int32, (rows, width), 1)
        for p in range(len(blocks)):
            limit = jnp.where(allowed[p] == 1, live[p], 0)
            reach = jnp.where(p == me, row, rows)
            bias[:, p * width : (p + 1) * width] = jnp.where(
                (col < limit) & (col <= reach), 0.0, NEG
            )

    peak[...] = jnp.full_like(peak, NEG)
    total[...] = jnp.zeros_like(total)
    for t in pairs:

        @pl.when(needed[t])
        def _():
            q = jnp.concatenate(
                [q_ref[:, g * HEAD_SIZE : (g + 1) * HEAD_SIZE] for g in range(group)], axis=0
            )
            keys = jnp.concatenate(
                [blocks[2 * t][:, :HEAD_SIZE], blocks[2 * t + 1][:, :HEAD_SIZE]], axis=0
            )
            part = lax.dot_general(
                q, keys, (((1,), (1,)), ((), ())), preferred_element_type=jnp.float32
            )
            part = part.reshape(group, rows, span) + bias[:, t * span : (t + 1) * span][None]
            part = part.reshape(group * rows, span)
            scores[:, t * span : (t + 1) * span] = part
            here = jnp.maximum(part[:, :width], part[:, width:])
            peak[...] = jnp.maximum(peak[...], here)

    top = jnp.max(peak[...], axis=1, keepdims=True)
    peak[...] = jnp.broadcast_to(top, peak.shape)
    for t in pairs:

        @pl.when(needed[t])
        def _():
            highest = jnp.concatenate([peak[...], peak[...]], axis=1)
            expo = jnp.exp2((scores[:, t * span : (t + 1) * span] - highest) * scale)
            vals = jnp.concatenate(
                [blocks[2 * t][:, HEAD_SIZE:], blocks[2 * t + 1][:, HEAD_SIZE:]], axis=0
            )
            both = jnp.concatenate([vals, jnp.ones((span, HEAD_SIZE), jnp.bfloat16)], axis=1)
            total[...] += jnp.dot(
                expo.astype(jnp.bfloat16), both, preferred_element_type=jnp.float32
            )

    alive = lax.broadcasted_iota(jnp.int32, (rows, HEAD_SIZE), 0) < live[me]
    for g in range(group):
        one = total[g * rows : (g + 1) * rows]
        out = jnp.where(alive, one[:, :HEAD_SIZE] / one[:, HEAD_SIZE:], 0.0)
        o_ref[:, g * HEAD_SIZE : (g + 1) * HEAD_SIZE] = out.astype(jnp.bfloat16)


def attend(mask, live, queries, first, heads, group, kv):
    rows = queries.shape[0]
    count, width = kv.shape[:2]
    step = group * HEAD_SIZE
    scale = HEAD_SIZE**-0.5 * 1.4426950408889634
    smem = pl.BlockSpec(memory_space=pltpu.SMEM)
    return pl.pallas_call(
        functools.partial(attend_kernel, scale),
        grid=(heads,),
        out_shape=jax.ShapeDtypeStruct((rows, heads * step), jnp.bfloat16),
        in_specs=[
            smem,
            smem,
            pl.BlockSpec((rows, step), lambda h: (0, first + h)),
            pl.BlockSpec((count, width, 2 * HEAD_SIZE), lambda h: (0, 0, h)),
        ],
        out_specs=pl.BlockSpec((rows, step), lambda h: (0, h)),
        scratch_shapes=[
            pltpu.VMEM((rows, count * width), jnp.float32),
            pltpu.VMEM((group * rows, count * width), jnp.float32),
            pltpu.VMEM((group * rows, width), jnp.float32),
            pltpu.VMEM((group * rows, 2 * HEAD_SIZE), jnp.float32),
        ],
        compiler_params=pltpu.CompilerParams(vmem_limit_bytes=40 * 2**20),
        cost_estimate=COST,
    )(mask, live, queries, kv)


def planar_kernel(scale, mask, live, q_ref, mine, theirs, o_ref):
    rows = q_ref.shape[0]
    group = q_ref.shape[1] // HEAD_SIZE
    chips, width = mine.shape[:2]
    me = lax.axis_index("seq")
    chip, core = me // 2, me % 2

    def body(n):
        slot = lax.broadcasted_iota(jnp.int32, (width, HEAD_SIZE), 0)
        zeroth = jnp.where(
            core == 0,
            mine[n - 1, :1, :HEAD_SIZE].astype(jnp.float32),
            theirs[n - 1, :1, :HEAD_SIZE].astype(jnp.float32),
        )
        zeroth = jnp.broadcast_to(zeroth, (width, HEAD_SIZE)).astype(jnp.bfloat16)
        keys, vals = [], []
        for j in range(n):
            r = (n - 1) ^ j
            for ref, block in ((mine, 2 * j + core), (theirs, 2 * j + 1 - core)):
                there = slot < jnp.where(mask[me, block] == 1, live[block], 0)
                if r == 0 and ref is mine:
                    keys.append(ref[r, :, :HEAD_SIZE])
                else:
                    keys.append(jnp.where(there, ref[r, :, :HEAD_SIZE], zeroth))
                vals.append(
                    jnp.concatenate(
                        [
                            jnp.where(there, ref[r, :, HEAD_SIZE:], jnp.bfloat16(0)),
                            jnp.where(there, jnp.bfloat16(1), jnp.bfloat16(0)),
                        ],
                        axis=1,
                    )
                )
        pairs = [jnp.concatenate(keys[2 * j : 2 * j + 2], axis=0) for j in range(n)]
        vals = jnp.concatenate(vals, axis=0)
        row = lax.broadcasted_iota(jnp.int32, (rows, width), 0)
        col = lax.broadcasted_iota(jnp.int32, (rows, width), 1)
        bias = jnp.where((col < live[me]) & (col <= row), 0.0, NEG)
        alive = lax.broadcasted_iota(jnp.int32, (rows, HEAD_SIZE), 0) < live[me]
        for g in range(group):
            cols = slice(g * HEAD_SIZE, (g + 1) * HEAD_SIZE)
            q = q_ref[:, cols]
            scores = []
            for j in range(n):
                part = lax.dot_general(
                    q, pairs[j], (((1,), (1,)), ((), ())), preferred_element_type=jnp.float32
                )
                own, other = part[:, :width], part[:, width:]
                scores += [own + bias if j == n - 1 else own, other]
            top = functools.reduce(jnp.maximum, scores)
            top = jnp.max(top, axis=1, keepdims=True)
            expo = [jnp.exp2((one - top) * scale).astype(jnp.bfloat16) for one in scores]
            out = jnp.dot(jnp.concatenate(expo, axis=1), vals, preferred_element_type=jnp.float32)
            out = jnp.where(alive, out[:, :HEAD_SIZE] / out[:, HEAD_SIZE:], 0.0)
            o_ref[:, cols] = out.astype(jnp.bfloat16)

    for n in range(1, chips + 1):
        pl.when(chip == n - 1)(functools.partial(body, n))


def attend_planar(mask, live, queries, first, group, mine, theirs, heads):
    rows = queries.shape[0]
    step = group * HEAD_SIZE
    smem = pl.BlockSpec(memory_space=pltpu.SMEM)
    kv = pl.BlockSpec(mine.shape[:2] + (2 * HEAD_SIZE,), lambda i: (0, 0, i))
    return pl.pallas_call(
        functools.partial(planar_kernel, HEAD_SIZE**-0.5 * 1.4426950408889634),
        grid=(heads,),
        out_shape=jax.ShapeDtypeStruct((rows, heads * step), jnp.bfloat16),
        in_specs=[smem, smem, pl.BlockSpec((rows, step), lambda i: (0, first + i)), kv, kv],
        out_specs=pl.BlockSpec((rows, step), lambda i: (0, i)),
        compiler_params=pltpu.CompilerParams(vmem_limit_bytes=40 * 2**20),
        cost_estimate=COST,
    )(mask, live, queries, mine, theirs)


def pack_heads(k_ref, v_ref, first, ref, count):
    for i in range(count):
        cols = slice((first + i) * HEAD_SIZE, (first + i + 1) * HEAD_SIZE)
        ref[:, 2 * i * HEAD_SIZE : (2 * i + 1) * HEAD_SIZE] = k_ref[:, cols]
        ref[:, (2 * i + 1) * HEAD_SIZE : (2 * i + 2) * HEAD_SIZE] = v_ref[:, cols]


def ahead_kernel(k_ref, v_ref, sent):
    pack_heads(k_ref, v_ref, 0, sent, sent.shape[1] // (2 * HEAD_SIZE))


def pack_ahead(keys, values, heads):
    rows = keys.shape[0]
    shape = (rows, heads * 2 * HEAD_SIZE)
    kv = whole((rows, heads * HEAD_SIZE))
    return pl.pallas_call(
        ahead_kernel,
        grid=(1,),
        out_shape=jax.ShapeDtypeStruct(shape, keys.dtype),
        in_specs=[kv, kv],
        out_specs=whole(shape),
        cost_estimate=COST,
    )(keys, values)


def rest_kernel(first, mask, live, q_ref, k_ref, v_ref, sent, q_sent, part):
    pack_heads(k_ref, v_ref, first, part, part.shape[1] // (2 * HEAD_SIZE))
    last = q_ref.shape[1]
    q_sent[:, :last] = q_ref[...]
    q_sent[:, last:] = jnp.zeros_like(q_sent[:, last:])
    blocks = live.shape[0]
    deep = 16
    row = lax.broadcasted_iota(jnp.int32, (deep, HEAD_SIZE), 0)
    col = lax.broadcasted_iota(jnp.int32, (deep, HEAD_SIZE), 1)
    tile = jnp.zeros((deep, HEAD_SIZE), jnp.int32)
    for j in range(blocks):
        tile = jnp.where((row == blocks) & (col == j), live[j], tile)
        for i in range(blocks):
            tile = jnp.where((row == i) & (col == j), mask[i, j], tile)
    q_sent[:deep, last:] = tile.astype(jnp.float32).astype(q_sent.dtype)


def whole(shape):
    return pl.BlockSpec(shape, lambda i: (0, 0))


def pack_rest(mask, live, queries, keys, values, first, sent):
    rows, cols = keys.shape
    q_cols = queries.shape[1] // (cols // HEAD_SIZE) * first
    smem = pl.BlockSpec(memory_space=pltpu.SMEM)
    shapes = [(rows, q_cols + HEAD_SIZE), (rows, 2 * (cols - first * HEAD_SIZE))]
    return pl.pallas_call(
        functools.partial(rest_kernel, first),
        grid=(1,),
        out_shape=[jax.ShapeDtypeStruct(shape, keys.dtype) for shape in shapes],
        in_specs=[smem, smem, whole((rows, q_cols)), whole(keys.shape), whole(values.shape)]
        + [pl.BlockSpec(memory_space=pl.ANY)],
        out_specs=[whole(shape) for shape in shapes],
        cost_estimate=COST,
    )(mask, live, queries, keys, values, sent)


def pack_pairs(keys, values, heads):
    parts = []
    for h in heads:
        cols = slice(h * HEAD_SIZE, (h + 1) * HEAD_SIZE)
        parts += [keys[:, cols], values[:, cols]]
    return jnp.concatenate(parts, axis=1)


def after(value, *others):
    return lax.optimization_barrier((value,) + others)[0] if others else value


def on_plane(nsec, to):
    return [(s * 8 + i, s * 8 + to(i)) for s in range(nsec) for i in range(8)]


def exchange(part, nsec, by):
    return lax.ppermute(part, ("section", "seq"), on_plane(nsec, lambda i: i ^ by))


def per_device_8(queries, keys, values, block_mask, block_live):
    nsec = lax.axis_size("section")
    kv_heads = keys.shape[2] // HEAD_SIZE
    group = queries.shape[2] // keys.shape[2]
    step = group * HEAD_SIZE
    q, k, v = queries[0], keys[0], values[0]
    mask, live = block_mask[0], block_live[0]
    onward = [(i, (i + 1) % nsec) for i in range(nsec)]
    half = kv_heads // 2

    def on(value):
        return lax.ppermute(value, "section", onward)

    def gather(part, count, *before):
        pieces = [part] + [exchange(part, nsec, by) for by in (2, 4)]
        pieces.append(exchange(after(part, *before), nsec, 6))
        width = part.shape[1] // count
        return [jnp.stack([p[:, i * width : (i + 1) * width] for p in pieces]) for i in range(count)]

    def both_cores(mines):
        return mines, [exchange(mine, nsec, 1) for mine in mines]

    def joined(arrays):
        return jnp.concatenate(arrays, axis=2) if len(arrays) > 1 else arrays[0]

    sent = pack_ahead(k, v, half)
    q_sent, part1 = pack_rest(mask, live, q, k, v, half, sent)
    sent_in, q_in = on(sent), on(q_sent)

    mines1 = gather(part1, 4, sent_in)
    kvs1 = [joined(arrays) for arrays in both_cores(mines1)]
    ctx = attend_planar(mask, live, q, half, group, *kvs1, half)
    out = on(ctx)

    part0 = after(sent_in, *mines1)
    mines0 = gather(part0, 2, ctx, q_in)
    mines0 = lax.optimization_barrier((*mines0, ctx))[:2]
    mines0, theirs0 = both_cores(mines0)
    blocks = live.shape[0]
    tab = q_in[: blocks + 1, half * step :][:, :blocks].astype(jnp.int32)
    mask_in, live_in = tab[:-1], tab[-1]
    heads = half // 2
    first = [
        attend_planar(mask_in, live_in, q_in, i * heads, group, mines0[i], theirs0[i], heads)
        for i in range(2)
    ]
    return jnp.concatenate(first + [out], axis=1)[None]


def per_device(queries, keys, values, block_mask, block_live):
    nsec = lax.axis_size("section")
    group = queries.shape[2] // keys.shape[2]
    onward = [(i, (i + 1) % nsec) for i in range(nsec)]
    outs = []
    for h in range(0, keys.shape[2] // HEAD_SIZE, 2):
        kv = lax.all_gather(pack_pairs(keys[0], values[0], [h, h + 1]), "seq", axis=0)
        out = attend(block_mask[0], block_live[0], queries[0], h, 2, group, kv)
        outs.append(lax.ppermute(out, "section", onward))
    return jnp.concatenate(outs, axis=1)[None]


def solution(mesh):
    placed = (
        P("section", "seq", None),
        P("section", "seq", None),
        P("section", "seq", None),
        P("section", None, None),
        P("section", None),
    )
    body = per_device_8 if mesh.shape["seq"] == 8 else per_device
    return jax.shard_map(
        body, mesh=mesh, in_specs=placed, out_specs=P("section", "seq", None), check_vma=False
    )
```

```python
import functools

import jax
import jax.numpy as jnp
from jax import lax
from jax.experimental import pallas as pl
from jax.experimental.pallas import tpu as pltpu
from jax.sharding import PartitionSpec as P

HEAD_SIZE = 128
NEG = -1e30
COST = pl.CostEstimate(flops=1, bytes_accessed=1, transcendentals=0)


def attend_kernel(scale, mask, live, q_ref, kv_ref, o_ref, bias, scores, peak, total):
    rows = q_ref.shape[0]
    group = q_ref.shape[1] // HEAD_SIZE
    blocks = [kv_ref.at[j] for j in range(kv_ref.shape[0])]
    width = blocks[0].shape[0]
    span = 2 * width
    me = lax.axis_index("seq")
    allowed = [mask[me, b] for b in range(len(blocks))]
    pairs = range(len(blocks) // 2)
    needed = [allowed[2 * t] + allowed[2 * t + 1] > 0 for t in pairs]

    @pl.when(pl.program_id(0) == 0)
    def _():
        row = lax.broadcasted_iota(jnp.int32, (rows, width), 0)
        col = lax.broadcasted_iota(jnp.int32, (rows, width), 1)
        for p in range(len(blocks)):
            limit = jnp.where(allowed[p] == 1, live[p], 0)
            reach = jnp.where(p == me, row, rows)
            bias[:, p * width : (p + 1) * width] = jnp.where(
                (col < limit) & (col <= reach), 0.0, NEG
            )

    peak[...] = jnp.full_like(peak, NEG)
    total[...] = jnp.zeros_like(total)
    for t in pairs:

        @pl.when(needed[t])
        def _():
            q = jnp.concatenate(
                [q_ref[:, g * HEAD_SIZE : (g + 1) * HEAD_SIZE] for g in range(group)], axis=0
            )
            keys = jnp.concatenate(
                [blocks[2 * t][:, :HEAD_SIZE], blocks[2 * t + 1][:, :HEAD_SIZE]], axis=0
            )
            part = lax.dot_general(
                q, keys, (((1,), (1,)), ((), ())), preferred_element_type=jnp.float32
            )
            part = part.reshape(group, rows, span) + bias[:, t * span : (t + 1) * span][None]
            part = part.reshape(group * rows, span)
            scores[:, t * span : (t + 1) * span] = part
            here = jnp.maximum(part[:, :width], part[:, width:])
            peak[...] = jnp.maximum(peak[...], here)

    top = jnp.max(peak[...], axis=1, keepdims=True)
    peak[...] = jnp.broadcast_to(top, peak.shape)
    for t in pairs:

        @pl.when(needed[t])
        def _():
            highest = jnp.concatenate([peak[...], peak[...]], axis=1)
            expo = jnp.exp2((scores[:, t * span : (t + 1) * span] - highest) * scale)
            vals = jnp.concatenate(
                [blocks[2 * t][:, HEAD_SIZE:], blocks[2 * t + 1][:, HEAD_SIZE:]], axis=0
            )
            both = jnp.concatenate([vals, jnp.ones((span, HEAD_SIZE), jnp.bfloat16)], axis=1)
            total[...] += jnp.dot(
                expo.astype(jnp.bfloat16), both, preferred_element_type=jnp.float32
            )

    alive = lax.broadcasted_iota(jnp.int32, (rows, HEAD_SIZE), 0) < live[me]
    for g in range(group):
        one = total[g * rows : (g + 1) * rows]
        out = jnp.where(alive, one[:, :HEAD_SIZE] / one[:, HEAD_SIZE:], 0.0)
        o_ref[:, g * HEAD_SIZE : (g + 1) * HEAD_SIZE] = out.astype(jnp.bfloat16)


def attend(mask, live, queries, first, heads, group, kv):
    rows = queries.shape[0]
    count, width = kv.shape[:2]
    step = group * HEAD_SIZE
    scale = HEAD_SIZE**-0.5 * 1.4426950408889634
    smem = pl.BlockSpec(memory_space=pltpu.SMEM)
    return pl.pallas_call(
        functools.partial(attend_kernel, scale),
        grid=(heads,),
        out_shape=jax.ShapeDtypeStruct((rows, heads * step), jnp.bfloat16),
        in_specs=[
            smem,
            smem,
            pl.BlockSpec((rows, step), lambda h: (0, first + h)),
            pl.BlockSpec((count, width, 2 * HEAD_SIZE), lambda h: (0, 0, h)),
        ],
        out_specs=pl.BlockSpec((rows, step), lambda h: (0, h)),
        scratch_shapes=[
            pltpu.VMEM((rows, count * width), jnp.float32),
            pltpu.VMEM((group * rows, count * width), jnp.float32),
            pltpu.VMEM((group * rows, width), jnp.float32),
            pltpu.VMEM((group * rows, 2 * HEAD_SIZE), jnp.float32),
        ],
        compiler_params=pltpu.CompilerParams(vmem_limit_bytes=40 * 2**20),
        cost_estimate=COST,
    )(mask, live, queries, kv)


def planar_kernel(scale, mask, live, q_ref, mine, theirs, o_ref):
    rows = q_ref.shape[0]
    group = q_ref.shape[1] // HEAD_SIZE
    chips, width = mine.shape[:2]
    me = lax.axis_index("seq")
    chip, core = me // 2, me % 2

    def body(n):
        slot = lax.broadcasted_iota(jnp.int32, (width, HEAD_SIZE), 0)
        zeroth = jnp.where(
            core == 0,
            mine[n - 1, :1, :HEAD_SIZE].astype(jnp.float32),
            theirs[n - 1, :1, :HEAD_SIZE].astype(jnp.float32),
        )
        zeroth = jnp.broadcast_to(zeroth, (width, HEAD_SIZE)).astype(jnp.bfloat16)
        keys, vals = [], []
        for j in range(n):
            r = (n - 1) ^ j
            for ref, block in ((mine, 2 * j + core), (theirs, 2 * j + 1 - core)):
                there = slot < jnp.where(mask[me, block] == 1, live[block], 0)
                if r == 0 and ref is mine:
                    keys.append(ref[r, :, :HEAD_SIZE])
                else:
                    keys.append(jnp.where(there, ref[r, :, :HEAD_SIZE], zeroth))
                vals.append(
                    jnp.concatenate(
                        [
                            jnp.where(there, ref[r, :, HEAD_SIZE:], jnp.bfloat16(0)),
                            jnp.where(there, jnp.bfloat16(1), jnp.bfloat16(0)),
                        ],
                        axis=1,
                    )
                )
        pairs = [jnp.concatenate(keys[2 * j : 2 * j + 2], axis=0) for j in range(n)]
        vals = jnp.concatenate(vals, axis=0)
        row = lax.broadcasted_iota(jnp.int32, (rows, width), 0)
        col = lax.broadcasted_iota(jnp.int32, (rows, width), 1)
        bias = jnp.where((col < live[me]) & (col <= row), 0.0, NEG)
        alive = lax.broadcasted_iota(jnp.int32, (rows, HEAD_SIZE), 0) < live[me]
        for g in range(group):
            cols = slice(g * HEAD_SIZE, (g + 1) * HEAD_SIZE)
            q = q_ref[:, cols]
            scores = []
            for j in range(n):
                part = lax.dot_general(
                    q, pairs[j], (((1,), (1,)), ((), ())), preferred_element_type=jnp.float32
                )
                own, other = part[:, :width], part[:, width:]
                scores += [own + bias if j == n - 1 else own, other]
            top = functools.reduce(jnp.maximum, scores)
            top = jnp.max(top, axis=1, keepdims=True)
            expo = [jnp.exp2((one - top) * scale).astype(jnp.bfloat16) for one in scores]
            out = jnp.dot(jnp.concatenate(expo, axis=1), vals, preferred_element_type=jnp.float32)
            out = jnp.where(alive, out[:, :HEAD_SIZE] / out[:, HEAD_SIZE:], 0.0)
            o_ref[:, cols] = out.astype(jnp.bfloat16)

    for n in range(1, chips + 1):
        pl.when(chip == n - 1)(functools.partial(body, n))


def attend_planar(mask, live, queries, first, group, mine, theirs, heads):
    rows = queries.shape[0]
    step = group * HEAD_SIZE
    smem = pl.BlockSpec(memory_space=pltpu.SMEM)
    kv = pl.BlockSpec(mine.shape[:2] + (2 * HEAD_SIZE,), lambda i: (0, 0, i))
    return pl.pallas_call(
        functools.partial(planar_kernel, HEAD_SIZE**-0.5 * 1.4426950408889634),
        grid=(heads,),
        out_shape=jax.ShapeDtypeStruct((rows, heads * step), jnp.bfloat16),
        in_specs=[smem, smem, pl.BlockSpec((rows, step), lambda i: (0, first + i)), kv, kv],
        out_specs=pl.BlockSpec((rows, step), lambda i: (0, i)),
        compiler_params=pltpu.CompilerParams(vmem_limit_bytes=40 * 2**20),
        cost_estimate=COST,
    )(mask, live, queries, mine, theirs)


def pack_heads(k_ref, v_ref, first, ref, count):
    for i in range(count):
        cols = slice((first + i) * HEAD_SIZE, (first + i + 1) * HEAD_SIZE)
        ref[:, 2 * i * HEAD_SIZE : (2 * i + 1) * HEAD_SIZE] = k_ref[:, cols]
        ref[:, (2 * i + 1) * HEAD_SIZE : (2 * i + 2) * HEAD_SIZE] = v_ref[:, cols]


def ahead_kernel(k_ref, v_ref, sent):
    pack_heads(k_ref, v_ref, 0, sent, sent.shape[1] // (2 * HEAD_SIZE))


def pack_ahead(keys, values, heads):
    rows = keys.shape[0]
    shape = (rows, heads * 2 * HEAD_SIZE)
    kv = whole((rows, heads * HEAD_SIZE))
    return pl.pallas_call(
        ahead_kernel,
        grid=(1,),
        out_shape=jax.ShapeDtypeStruct(shape, keys.dtype),
        in_specs=[kv, kv],
        out_specs=whole(shape),
        cost_estimate=COST,
    )(keys, values)


def rest_kernel(first, mask, live, q_ref, k_ref, v_ref, sent, q_sent, part):
    pack_heads(k_ref, v_ref, first, part, part.shape[1] // (2 * HEAD_SIZE))
    last = q_ref.shape[1]
    q_sent[:, :last] = q_ref[...]
    q_sent[:, last:] = jnp.zeros_like(q_sent[:, last:])
    blocks = live.shape[0]
    deep = 16
    row = lax.broadcasted_iota(jnp.int32, (deep, HEAD_SIZE), 0)
    col = lax.broadcasted_iota(jnp.int32, (deep, HEAD_SIZE), 1)
    tile = jnp.zeros((deep, HEAD_SIZE), jnp.int32)
    for j in range(blocks):
        tile = jnp.where((row == blocks) & (col == j), live[j], tile)
        for i in range(blocks):
            tile = jnp.where((row == i) & (col == j), mask[i, j], tile)
    q_sent[:deep, last:] = tile.astype(jnp.float32).astype(q_sent.dtype)


def whole(shape):
    return pl.BlockSpec(shape, lambda i: (0, 0))


def pack_rest(mask, live, queries, keys, values, first, sent):
    rows, cols = keys.shape
    q_cols = queries.shape[1] // (cols // HEAD_SIZE) * first
    smem = pl.BlockSpec(memory_space=pltpu.SMEM)
    shapes = [(rows, q_cols + HEAD_SIZE), (rows, 2 * (cols - first * HEAD_SIZE))]
    return pl.pallas_call(
        functools.partial(rest_kernel, first),
        grid=(1,),
        out_shape=[jax.ShapeDtypeStruct(shape, keys.dtype) for shape in shapes],
        in_specs=[smem, smem, whole((rows, q_cols)), whole(keys.shape), whole(values.shape)]
        + [pl.BlockSpec(memory_space=pl.ANY)],
        out_specs=[whole(shape) for shape in shapes],
        cost_estimate=COST,
    )(mask, live, queries, keys, values, sent)


def pack_pairs(keys, values, heads):
    parts = []
    for h in heads:
        cols = slice(h * HEAD_SIZE, (h + 1) * HEAD_SIZE)
        parts += [keys[:, cols], values[:, cols]]
    return jnp.concatenate(parts, axis=1)


def after(value, *others):
    return lax.optimization_barrier((value,) + others)[0] if others else value


def on_plane(nsec, to):
    return [(s * 8 + i, s * 8 + to(i)) for s in range(nsec) for i in range(8)]


def exchange(part, nsec, by):
    return lax.ppermute(part, ("section", "seq"), on_plane(nsec, lambda i: i ^ by))


def per_device_8(queries, keys, values, block_mask, block_live):
    nsec = lax.axis_size("section")
    kv_heads = keys.shape[2] // HEAD_SIZE
    group = queries.shape[2] // keys.shape[2]
    step = group * HEAD_SIZE
    q, k, v = queries[0], keys[0], values[0]
    mask, live = block_mask[0], block_live[0]
    onward = [(i, (i + 1) % nsec) for i in range(nsec)]
    half = kv_heads // 2

    def on(value):
        return lax.ppermute(value, "section", onward)

    def gather(part, count, *before):
        pieces = [part] + [exchange(part, nsec, by) for by in (2, 4)]
        pieces.append(exchange(after(part, *before), nsec, 6))
        width = part.shape[1] // count
        return [jnp.stack([p[:, i * width : (i + 1) * width] for p in pieces]) for i in range(count)]

    def both_cores(mines):
        return mines, [exchange(mine, nsec, 1) for mine in mines]

    def joined(arrays):
        return jnp.concatenate(arrays, axis=2) if len(arrays) > 1 else arrays[0]

    sent = pack_ahead(k, v, half)
    q_sent, part1 = pack_rest(mask, live, q, k, v, half, sent)
    sent_in, q_in = on(sent), on(q_sent)

    mines1 = gather(part1, 4, sent_in)
    kvs1 = [joined(arrays) for arrays in both_cores(mines1)]
    ctx = attend_planar(mask, live, q, half, group, *kvs1, half)
    out = on(ctx)

    part0 = after(sent_in, *mines1)
    mines0 = gather(part0, 4, ctx, q_in)
    mines0 = lax.optimization_barrier((*mines0, ctx))[:4]
    mines0, theirs0 = both_cores(mines0)
    blocks = live.shape[0]
    tab = q_in[: blocks + 1, half * step :][:, :blocks].astype(jnp.int32)
    mask_in, live_in = tab[:-1], tab[-1]
    first = [attend_planar(mask_in, live_in, q_in, 0, group, joined(mines0), joined(theirs0), half)]
    held = jnp.concatenate(first + [jnp.zeros_like(out)], axis=1)
    return lax.dynamic_update_slice(lax.optimization_barrier(held), out, (0, half * step))[None]


def per_device(queries, keys, values, block_mask, block_live):
    nsec = lax.axis_size("section")
    group = queries.shape[2] // keys.shape[2]
    onward = [(i, (i + 1) % nsec) for i in range(nsec)]
    outs = []
    for h in range(0, keys.shape[2] // HEAD_SIZE, 2):
        kv = lax.all_gather(pack_pairs(keys[0], values[0], [h, h + 1]), "seq", axis=0)
        out = attend(block_mask[0], block_live[0], queries[0], h, 2, group, kv)
        outs.append(lax.ppermute(out, "section", onward))
    return jnp.concatenate(outs, axis=1)[None]


def solution(mesh):
    placed = (
        P("section", "seq", None),
        P("section", "seq", None),
        P("section", "seq", None),
        P("section", None, None),
        P("section", None),
    )
    body = per_device_8 if mesh.shape["seq"] == 8 else per_device
    return jax.shard_map(
        body, mesh=mesh, in_specs=placed, out_specs=P("section", "seq", None), check_vma=False
    )
```

```python
import functools

import jax
import jax.numpy as jnp
from jax import lax
from jax.experimental import pallas as pl
from jax.experimental.pallas import tpu as pltpu
from jax.sharding import PartitionSpec as P

HEAD_SIZE = 128
NEG = -1e30
COST = pl.CostEstimate(flops=1, bytes_accessed=1, transcendentals=0)


def attend_kernel(scale, mask, live, q_ref, kv_ref, o_ref, bias, scores, peak, total):
    rows = q_ref.shape[0]
    group = q_ref.shape[1] // HEAD_SIZE
    blocks = [kv_ref.at[j] for j in range(kv_ref.shape[0])]
    width = blocks[0].shape[0]
    span = 2 * width
    me = lax.axis_index("seq")
    allowed = [mask[me, b] for b in range(len(blocks))]
    pairs = range(len(blocks) // 2)
    needed = [allowed[2 * t] + allowed[2 * t + 1] > 0 for t in pairs]

    @pl.when(pl.program_id(0) == 0)
    def _():
        row = lax.broadcasted_iota(jnp.int32, (rows, width), 0)
        col = lax.broadcasted_iota(jnp.int32, (rows, width), 1)
        for p in range(len(blocks)):
            limit = jnp.where(allowed[p] == 1, live[p], 0)
            reach = jnp.where(p == me, row, rows)
            bias[:, p * width : (p + 1) * width] = jnp.where(
                (col < limit) & (col <= reach), 0.0, NEG
            )

    peak[...] = jnp.full_like(peak, NEG)
    total[...] = jnp.zeros_like(total)
    for t in pairs:

        @pl.when(needed[t])
        def _():
            q = jnp.concatenate(
                [q_ref[:, g * HEAD_SIZE : (g + 1) * HEAD_SIZE] for g in range(group)], axis=0
            )
            keys = jnp.concatenate(
                [blocks[2 * t][:, :HEAD_SIZE], blocks[2 * t + 1][:, :HEAD_SIZE]], axis=0
            )
            part = lax.dot_general(
                q, keys, (((1,), (1,)), ((), ())), preferred_element_type=jnp.float32
            )
            part = part.reshape(group, rows, span) + bias[:, t * span : (t + 1) * span][None]
            part = part.reshape(group * rows, span)
            scores[:, t * span : (t + 1) * span] = part
            here = jnp.maximum(part[:, :width], part[:, width:])
            peak[...] = jnp.maximum(peak[...], here)

    top = jnp.max(peak[...], axis=1, keepdims=True)
    peak[...] = jnp.broadcast_to(top, peak.shape)
    for t in pairs:

        @pl.when(needed[t])
        def _():
            highest = jnp.concatenate([peak[...], peak[...]], axis=1)
            expo = jnp.exp2((scores[:, t * span : (t + 1) * span] - highest) * scale)
            vals = jnp.concatenate(
                [blocks[2 * t][:, HEAD_SIZE:], blocks[2 * t + 1][:, HEAD_SIZE:]], axis=0
            )
            both = jnp.concatenate([vals, jnp.ones((span, HEAD_SIZE), jnp.bfloat16)], axis=1)
            total[...] += jnp.dot(
                expo.astype(jnp.bfloat16), both, preferred_element_type=jnp.float32
            )

    alive = lax.broadcasted_iota(jnp.int32, (rows, HEAD_SIZE), 0) < live[me]
    for g in range(group):
        one = total[g * rows : (g + 1) * rows]
        out = jnp.where(alive, one[:, :HEAD_SIZE] / one[:, HEAD_SIZE:], 0.0)
        o_ref[:, g * HEAD_SIZE : (g + 1) * HEAD_SIZE] = out.astype(jnp.bfloat16)


def attend(mask, live, queries, first, heads, group, kv):
    rows = queries.shape[0]
    count, width = kv.shape[:2]
    step = group * HEAD_SIZE
    scale = HEAD_SIZE**-0.5 * 1.4426950408889634
    smem = pl.BlockSpec(memory_space=pltpu.SMEM)
    return pl.pallas_call(
        functools.partial(attend_kernel, scale),
        grid=(heads,),
        out_shape=jax.ShapeDtypeStruct((rows, heads * step), jnp.bfloat16),
        in_specs=[
            smem,
            smem,
            pl.BlockSpec((rows, step), lambda h: (0, first + h)),
            pl.BlockSpec((count, width, 2 * HEAD_SIZE), lambda h: (0, 0, h)),
        ],
        out_specs=pl.BlockSpec((rows, step), lambda h: (0, h)),
        scratch_shapes=[
            pltpu.VMEM((rows, count * width), jnp.float32),
            pltpu.VMEM((group * rows, count * width), jnp.float32),
            pltpu.VMEM((group * rows, width), jnp.float32),
            pltpu.VMEM((group * rows, 2 * HEAD_SIZE), jnp.float32),
        ],
        compiler_params=pltpu.CompilerParams(vmem_limit_bytes=40 * 2**20),
        cost_estimate=COST,
    )(mask, live, queries, kv)


def planar_kernel(scale, mask, live, q_ref, mine, theirs, o_ref):
    rows = q_ref.shape[0]
    group = q_ref.shape[1] // HEAD_SIZE
    chips, width = mine.shape[:2]
    me = lax.axis_index("seq")
    chip, core = me // 2, me % 2

    def body(n):
        slot = lax.broadcasted_iota(jnp.int32, (width, HEAD_SIZE), 0)
        zeroth = jnp.where(
            core == 0,
            mine[n - 1, :1, :HEAD_SIZE].astype(jnp.float32),
            theirs[n - 1, :1, :HEAD_SIZE].astype(jnp.float32),
        )
        zeroth = jnp.broadcast_to(zeroth, (width, HEAD_SIZE)).astype(jnp.bfloat16)
        keys, vals = [], []
        for j in range(n):
            r = (n - 1) ^ j
            for ref, block in ((mine, 2 * j + core), (theirs, 2 * j + 1 - core)):
                there = slot < jnp.where(mask[me, block] == 1, live[block], 0)
                if r == 0 and ref is mine:
                    keys.append(ref[r, :, :HEAD_SIZE])
                else:
                    keys.append(jnp.where(there, ref[r, :, :HEAD_SIZE], zeroth))
                vals.append(
                    jnp.concatenate(
                        [
                            jnp.where(there, ref[r, :, HEAD_SIZE:], jnp.bfloat16(0)),
                            jnp.where(there, jnp.bfloat16(1), jnp.bfloat16(0)),
                        ],
                        axis=1,
                    )
                )
        pairs = [jnp.concatenate(keys[2 * j : 2 * j + 2], axis=0) for j in range(n)]
        vals = jnp.concatenate(vals, axis=0)
        row = lax.broadcasted_iota(jnp.int32, (rows, width), 0)
        col = lax.broadcasted_iota(jnp.int32, (rows, width), 1)
        bias = jnp.where((col < live[me]) & (col <= row), 0.0, NEG)
        alive = lax.broadcasted_iota(jnp.int32, (rows, HEAD_SIZE), 0) < live[me]
        for g in range(group):
            cols = slice(g * HEAD_SIZE, (g + 1) * HEAD_SIZE)
            q = q_ref[:, cols]
            scores = []
            for j in range(n):
                part = lax.dot_general(
                    q, pairs[j], (((1,), (1,)), ((), ())), preferred_element_type=jnp.float32
                )
                own, other = part[:, :width], part[:, width:]
                scores += [own + bias if j == n - 1 else own, other]
            top = functools.reduce(jnp.maximum, scores)
            top = jnp.max(top, axis=1, keepdims=True)
            expo = [jnp.exp2((one - top) * scale).astype(jnp.bfloat16) for one in scores]
            out = jnp.dot(jnp.concatenate(expo, axis=1), vals, preferred_element_type=jnp.float32)
            out = jnp.where(alive, out[:, :HEAD_SIZE] / out[:, HEAD_SIZE:], 0.0)
            o_ref[:, cols] = out.astype(jnp.bfloat16)

    for n in range(1, chips + 1):
        pl.when(chip == n - 1)(functools.partial(body, n))


def attend_planar(mask, live, queries, first, group, mine, theirs, heads):
    rows = queries.shape[0]
    step = group * HEAD_SIZE
    smem = pl.BlockSpec(memory_space=pltpu.SMEM)
    kv = pl.BlockSpec(mine.shape[:2] + (2 * HEAD_SIZE,), lambda i: (0, 0, i))
    return pl.pallas_call(
        functools.partial(planar_kernel, HEAD_SIZE**-0.5 * 1.4426950408889634),
        grid=(heads,),
        out_shape=jax.ShapeDtypeStruct((rows, heads * step), jnp.bfloat16),
        in_specs=[smem, smem, pl.BlockSpec((rows, step), lambda i: (0, first + i)), kv, kv],
        out_specs=pl.BlockSpec((rows, step), lambda i: (0, i)),
        compiler_params=pltpu.CompilerParams(vmem_limit_bytes=40 * 2**20),
        cost_estimate=COST,
    )(mask, live, queries, mine, theirs)


def pack_heads(k_ref, v_ref, first, ref, count):
    for i in range(count):
        cols = slice((first + i) * HEAD_SIZE, (first + i + 1) * HEAD_SIZE)
        ref[:, 2 * i * HEAD_SIZE : (2 * i + 1) * HEAD_SIZE] = k_ref[:, cols]
        ref[:, (2 * i + 1) * HEAD_SIZE : (2 * i + 2) * HEAD_SIZE] = v_ref[:, cols]


def ahead_kernel(k_ref, v_ref, sent):
    pack_heads(k_ref, v_ref, 0, sent, sent.shape[1] // (2 * HEAD_SIZE))


def pack_ahead(keys, values, heads):
    rows = keys.shape[0]
    shape = (rows, heads * 2 * HEAD_SIZE)
    kv = whole((rows, heads * HEAD_SIZE))
    return pl.pallas_call(
        ahead_kernel,
        grid=(1,),
        out_shape=jax.ShapeDtypeStruct(shape, keys.dtype),
        in_specs=[kv, kv],
        out_specs=whole(shape),
        cost_estimate=COST,
    )(keys, values)


def rest_kernel(first, mask, live, k_ref, v_ref, sent, *refs):
    q_refs, (q_sent, part) = refs[:-2], refs[-2:]
    pack_heads(k_ref, v_ref, first, part, part.shape[1] // (2 * HEAD_SIZE))
    step = q_refs[0].shape[1]
    last = step * len(q_refs)
    for i, ref in enumerate(q_refs):
        q_sent[:, i * step : (i + 1) * step] = ref[...]
    q_sent[:, last:] = jnp.zeros_like(q_sent[:, last:])
    blocks = live.shape[0]
    deep = 16
    row = lax.broadcasted_iota(jnp.int32, (deep, HEAD_SIZE), 0)
    col = lax.broadcasted_iota(jnp.int32, (deep, HEAD_SIZE), 1)
    place = jnp.where(col < blocks, row * blocks + col, -1)
    tile = jnp.zeros((deep, HEAD_SIZE), jnp.int32)
    for j in range(blocks):
        tile = jnp.where(place == blocks * blocks + j, live[j], tile)
        for i in range(blocks):
            tile = jnp.where(place == i * blocks + j, mask[i, j], tile)
    q_sent[:deep, last:] = tile.astype(jnp.float32).astype(q_sent.dtype)


def whole(shape):
    return pl.BlockSpec(shape, lambda i: (0, 0))


def pack_rest(mask, live, queries, keys, values, first, sent):
    rows, cols = keys.shape
    q_cols = queries.shape[1] // (cols // HEAD_SIZE) * first
    smem = pl.BlockSpec(memory_space=pltpu.SMEM)
    shapes = [(rows, q_cols + HEAD_SIZE), (rows, 2 * (cols - first * HEAD_SIZE))]
    return pl.pallas_call(
        functools.partial(rest_kernel, first),
        grid=(1,),
        out_shape=[jax.ShapeDtypeStruct(shape, keys.dtype) for shape in shapes],
        in_specs=[smem, smem, whole(keys.shape), whole(values.shape)]
        + [pl.BlockSpec(memory_space=pl.ANY)]
        + [pl.BlockSpec((rows, q_cols // first), lambda i, at=at: (0, at)) for at in range(first)],
        out_specs=[whole(shape) for shape in shapes],
        cost_estimate=COST,
    )(mask, live, keys, values, sent, *[queries] * first)


def pack_pairs(keys, values, heads):
    parts = []
    for h in heads:
        cols = slice(h * HEAD_SIZE, (h + 1) * HEAD_SIZE)
        parts += [keys[:, cols], values[:, cols]]
    return jnp.concatenate(parts, axis=1)


def after(value, *others):
    return lax.optimization_barrier((value,) + others)[0] if others else value


def on_plane(nsec, to):
    return [(s * 8 + i, s * 8 + to(i)) for s in range(nsec) for i in range(8)]


def exchange(part, nsec, by):
    return lax.ppermute(part, ("section", "seq"), on_plane(nsec, lambda i: i ^ by))


def per_device_8(queries, keys, values, block_mask, block_live):
    nsec = lax.axis_size("section")
    kv_heads = keys.shape[2] // HEAD_SIZE
    group = queries.shape[2] // keys.shape[2]
    step = group * HEAD_SIZE
    q, k, v = queries[0], keys[0], values[0]
    mask, live = block_mask[0], block_live[0]
    onward = [(i, (i + 1) % nsec) for i in range(nsec)]
    half = kv_heads // 2

    def on(value):
        return lax.ppermute(value, "section", onward)

    def gather(part, count, *before):
        pieces = [part] + [exchange(part, nsec, by) for by in (2, 4)]
        pieces.append(exchange(after(part, *before), nsec, 6))
        width = part.shape[1] // count
        return [jnp.stack([p[:, i * width : (i + 1) * width] for p in pieces]) for i in range(count)]

    def both_cores(mines):
        return mines, [exchange(mine, nsec, 1) for mine in mines]

    def joined(arrays):
        return jnp.concatenate(arrays, axis=2) if len(arrays) > 1 else arrays[0]

    sent = pack_ahead(k, v, half)
    q_sent, part1 = pack_rest(mask, live, q, k, v, half, sent)
    sent_in, q_in = on(sent), on(q_sent)

    mines1 = gather(part1, 4, sent_in)
    kvs1 = [joined(arrays) for arrays in both_cores(mines1)]
    ctx = attend_planar(mask, live, q, half, group, *kvs1, half)
    out = on(ctx)

    part0 = after(sent_in, *mines1)
    mines0 = gather(part0, 4, ctx, q_in)
    mines0 = lax.optimization_barrier((*mines0, ctx))[:4]
    mines0, theirs0 = both_cores(mines0)
    blocks = live.shape[0]
    tab = q_in[: blocks + 1, half * step :][:, :blocks].astype(jnp.int32)
    mask_in, live_in = tab[:-1], tab[-1]
    first = [attend_planar(mask_in, live_in, q_in, 0, group, joined(mines0), joined(theirs0), half)]
    held = jnp.concatenate(first + [jnp.zeros_like(out)], axis=1)
    return lax.dynamic_update_slice(lax.optimization_barrier(held), out, (0, half * step))[None]


def per_device(queries, keys, values, block_mask, block_live):
    nsec = lax.axis_size("section")
    group = queries.shape[2] // keys.shape[2]
    onward = [(i, (i + 1) % nsec) for i in range(nsec)]
    outs = []
    for h in range(0, keys.shape[2] // HEAD_SIZE, 2):
        kv = lax.all_gather(pack_pairs(keys[0], values[0], [h, h + 1]), "seq", axis=0)
        out = attend(block_mask[0], block_live[0], queries[0], h, 2, group, kv)
        outs.append(lax.ppermute(out, "section", onward))
    return jnp.concatenate(outs, axis=1)[None]


def solution(mesh):
    placed = (
        P("section", "seq", None),
        P("section", "seq", None),
        P("section", "seq", None),
        P("section", None, None),
        P("section", None),
    )
    body = per_device_8 if mesh.shape["seq"] == 8 else per_device
    return jax.shard_map(
        body, mesh=mesh, in_specs=placed, out_specs=P("section", "seq", None), check_vma=False
    )
```
